32 devices in a mesh: dp: 16 (over z, y, x), tensor: 2 (over core).
Axes of the slice: x: 2, y: 2, z: 4, core: 2. Of those that a mesh axis runs over, the one named last changes fastest.
Arguments:
- hidden_in: bfloat16 [4096, 768], P(('dp', 'tensor')), may hold values from -6 to 6
- norm1_gain: float32 [768], replicated, may hold values from 0.1 to 1.9
- q_weight: bfloat16 [768, 768], P('dp', 'tensor'), may hold values from -0.21875 to 0.21875
- k_weight: bfloat16 [768, 768], P('dp', 'tensor'), may hold values from -0.21875 to 0.21875
- v_weight: bfloat16 [768, 768], P('dp', 'tensor'), may hold values from -0.21875 to 0.21875
- out_weight: bfloat16 [768, 768], P('tensor', 'dp'), may hold values from -0.875 to 0.875
- position_bias: float32 [32, 12], P(None, 'tensor'), may hold values from -4 to 4
- norm2_gain: float32 [768], replicated, may hold values from 0.1 to 1.9
- router_weight: float32 [768, 8], replicated, may hold values from -0.15625 to 0.15625
- expert_up: bfloat16 [16, 768, 1536], P('dp', None, 'tensor'), may hold values from -0.21875 to 0.21875
- expert_down: bfloat16 [16, 1536, 768], P('dp', 'tensor'), may hold values from -6 to 6
- doc_lengths: int32 [16, 4], P('dp'), may hold values from 1 to 128, as said below
- expert_route: int32 [4096, 1], P('dp'), may hold values from 0 to 7; in each aligned block of 256 rows (0 to 255, 256 to 511, ...) at most 40 rows name the same one
- out_grad: bfloat16 [4096, 768], P(('dp', 'tensor')), may hold values from -6 to 6
Outputs:
- hidden_out: bfloat16 [4096, 768], P(('dp', 'tensor'))
- input_grad: float32 [4096, 768], P(('dp', 'tensor'))
- norm1_gain_grad: float32 [768], replicated
- q_weight_grad: float32 [768, 768], P('dp', 'tensor')
- k_weight_grad: float32 [768, 768], P('dp', 'tensor')
- v_weight_grad: float32 [768, 768], P('dp', 'tensor')
- out_weight_grad: float32 [768, 768], P('tensor', 'dp')
- position_bias_grad: float32 [32, 12], P(None, 'tensor')
- norm2_gain_grad: float32 [768], replicated
- router_weight_grad: float32 [768, 8], replicated
- expert_up_grad: float32 [16, 768, 1536], P('dp', None, 'tensor')
- expert_down_grad: float32 [16, 1536, 768], P('dp', 'tensor')
The draws below stay inside these ranges and needn't reach their ends.
Inputs may be any that keep to these rules, and one draw needn't show every extreme that they name: `doc_lengths`: the 4 lengths of a group sum to 256; the second document is exactly 128 long and holds the group's rows 127 and 128; the first is 32 to 96 long. `expert_route`: within one group's 256 rows no expert is named by more than 40 rows.
All inputs are finite; a program needn't handle non-finite values.
Results may differ from the reference program's by a relative error of at most 0.023.
Values may be sent and summed in bfloat16 or wider, within the bound.
A program may use at most 128 MiB of HBM per device.

```python
import math
from functools import partial
import jax
import jax.numpy as jnp
import numpy as np
from jax import lax

D = 768
HEADS = 12
DH = 64
FF = 3072
BUCKETS = 32
TOK_DP = 256
EXPERTS = 8
CAP = 40
TOKENS = 4096
N_DP = 16


def draw_doc_lengths(key, part):
    key = jax.random.fold_in(key, 11)
    first_key, second_key = jax.random.split(key)
    half_group = TOK_DP // 2
    eighth = TOK_DP // 8
    leading = jax.random.randint(first_key, (N_DP,), eighth, 3 * eighth + 1).astype(jnp.int32)
    trailing = half_group - leading
    third_length = jax.random.randint(second_key, (N_DP,), 0, 1 << 30).astype(jnp.int32) % (trailing - 1) + 1
    fourth = trailing - third_length
    middle = jnp.full((N_DP,), half_group, jnp.int32)
    return jnp.stack([leading, middle, third_length, fourth], axis=1).astype(jnp.int32)


def level_of(own_key, extent, cuts, least, largest):
    def one(axis_at, blocks):
        steps = jax.random.uniform(jax.random.fold_in(jax.random.fold_in(own_key, 6), axis_at), (blocks,), jnp.float32, least / len(cuts), largest / len(cuts))
        return jnp.repeat(jnp.exp(steps), extent[axis_at] // blocks).reshape((-1,) + (1,) * (len(extent) - axis_at - 1))

    loudness = one(*cuts[0])
    for cut in cuts[1:]:
        loudness = loudness * one(*cut)
    return loudness


def shared_out(key, own, number, rows, count, top, reach, lean):
    order = jax.random.permutation(key, count)
    crowded, common = shares(count, rows * top, reach, lean, True), shares(count, rows * top, reach, lean, False)
    places = jnp.arange(count)

    def named(sizes, offset_by):
        used = int((sizes > 0).sum())
        fixed = max(1, used // 4)
        shifted = fixed + (places - fixed + offset_by * (used - fixed)) % max(1, count - fixed)
        return jnp.zeros((count,), jnp.int32).at[order[jnp.where(places < fixed, places, shifted)]].set(jnp.asarray(sizes, jnp.int32))

    sizes = jnp.where(number % 4 == 0, named(crowded, number // 4), named(common, number - number // 4 - 1))
    mixed = jax.random.permutation(jax.random.fold_in(own, 3), count)
    giver, sink = mixed[0:count // 2 * 2:2], mixed[1:count // 2 * 2:2]
    margin = jnp.minimum(sizes[giver] - 1, reach - sizes[sink]) // 2
    margin = jnp.where((giver == order[0]) | (sink == order[0]) | (sizes[sink] == 0), 0, jnp.maximum(margin, 0))
    shifted = jax.random.randint(jax.random.fold_in(own, 4), (count // 2,), 0, 1 << 20) % (margin + 1)
    sizes = sizes.at[giver].add(-shifted).at[sink].add(shifted)
    members = jnp.searchsorted(jnp.cumsum(sizes), jnp.arange(rows * top), side="right").astype(jnp.int32)
    table = members.reshape(top, rows).T
    table = table[jax.random.permutation(jax.random.fold_in(own, 1), rows)]
    offset_by = jax.random.randint(jax.random.fold_in(own, 2), (rows, 1), 0, top)
    return jnp.take_along_axis(table, (jnp.arange(top)[None, :] + offset_by) % top, axis=1)


def shares(count, total, bound, lean, full):
    portions = [(1 << 20) // math.isqrt(grade ** lean) + 1 for grade in range(1, count + 1)]
    largest = bound if full else min(bound, max(-(-total // count), total * portions[0] // sum(portions)))
    least = 1 if total - largest >= count - 1 else 0
    holding, spare = [largest] + [least] * (count - 1), total - largest - least * (count - 1)
    while spare > 0:
        candidates = [i for i in range(1, count) if holding[i] < largest] or [i for i in range(1, count) if holding[i] < bound]
        mass, remaining = sum([portions[i] for i in candidates]), spare
        for i in candidates:
            more = min(bound - holding[i], max(1, remaining * portions[i] // mass), spare)
            holding[i] = holding[i] + more
            spare = spare - more
    return np.array(holding)


def bell_draw(rng, dims, deviation, bound, shards=(), kind=jnp.bfloat16):
    drawn = deviation * jax.random.normal(rng, dims, jnp.float32)
    if shards:
        drawn = drawn * level_of(rng, dims, shards, -0.22, 0.18)
    return jnp.clip(drawn, -bound, bound).astype(kind)


def setup_inputs(seed: int = 0) -> dict:
    keys = jax.random.split(jax.random.key(seed), 15)
    hidden_in = bell_draw(keys[0], (TOKENS, D), 1.0, 6.0, ((0, 32),))
    norm1_gain = jnp.clip(1.0 + 0.18 * jax.random.normal(keys[1], (D,), jnp.float32), 0.1, 1.9)
    q_weight = bell_draw(keys[2], (D, HEADS * DH), D ** -0.5, 0.21875, ((0, 16), (1, 2)))
    k_weight = bell_draw(keys[3], (D, HEADS * DH), D ** -0.5, 0.21875, ((0, 16), (1, 2)))
    v_weight = bell_draw(keys[4], (D, HEADS * DH), D ** -0.5, 0.21875, ((0, 16), (1, 2)))
    out_weight = bell_draw(keys[5], (HEADS * DH, D), (max(1, D // 16)) ** -0.5, 0.875, ((0, 2), (1, 16)))
    position_bias = bell_draw(keys[6], (BUCKETS, HEADS), 1.0, 4.0, ((1, 2),), jnp.float32)
    norm2_gain = jnp.clip(1.0 + 0.18 * jax.random.normal(keys[7], (D,), jnp.float32), 0.1, 1.9)
    router_weight = bell_draw(keys[8], (D, EXPERTS), (2 * D) ** -0.5, 0.15625, (), jnp.float32)
    expert_up = bell_draw(keys[9], (2 * EXPERTS, D, FF // 2), D ** -0.5, 0.21875, ((0, 16), (2, 2)))
    expert_down = bell_draw(keys[10], (2 * EXPERTS, FF // 2, D), (max(1, FF // 2048)) ** -0.5, 6.0, ((0, 16), (1, 2)))
    doc_lengths = draw_doc_lengths(jax.random.fold_in(keys[14], 71), 0)
    expert_route_keys = jax.random.split(jax.random.fold_in(keys[12], 1), TOKENS // TOK_DP)
    expert_route_turns = jax.random.permutation(jax.random.fold_in(keys[12], 3), TOKENS // TOK_DP)
    expert_route = jax.vmap(lambda own, number: shared_out(jax.random.fold_in(keys[12], 2), own, number, TOK_DP, EXPERTS, 1, CAP, 1))(expert_route_keys, expert_route_turns).reshape((TOKENS, 1))
    out_grad = bell_draw(keys[13], (TOKENS, D), 1.0, 6.0, ((0, 32),))
    return dict(hidden_in=hidden_in, norm1_gain=norm1_gain, q_weight=q_weight, k_weight=k_weight, v_weight=v_weight, out_weight=out_weight, position_bias=position_bias, norm2_gain=norm2_gain, router_weight=router_weight, expert_up=expert_up, expert_down=expert_down, doc_lengths=doc_lengths, expert_route=expert_route, out_grad=out_grad)


@jax.custom_vjp
def low(v):
    return lax.optimization_barrier(v.astype(jnp.bfloat16)).astype(jnp.float32)

@jax.custom_vjp
def low_back(v):
    return v

def low_keep(v):
    return (low(v), None)

def low_pass(kept, grad):
    return (grad,)

def back_keep(v):
    return (v, None)

def back_low(kept, grad):
    return (low(grad),)
low.defvjp(low_keep, low_pass)
low_back.defvjp(back_keep, back_low)
EPSILON = 1e-06
NEGATIVE = -1e+30
LIMITS = (12, 16, 23, 32, 46, 64, 91)

def matrix_product(first_operand, second_operand):
    return jnp.dot(first_operand, second_operand, precision=lax.Precision.HIGHEST, preferred_element_type=jnp.float32)

def rms_norm(values, gain_vector):
    return values * lax.rsqrt(lax.optimization_barrier(jnp.mean(values * values, axis=-1, keepdims=True)) + EPSILON) * gain_vector

def bucket_of(offset):
    distance = jnp.abs(offset)
    beyond = jnp.zeros_like(distance)
    for boundary in LIMITS:
        beyond = beyond + (distance >= boundary).astype(jnp.int32)
    near_far = jnp.where(distance < 8, distance, 8 + beyond)
    return (near_far + 16 * (offset > 0).astype(jnp.int32)).astype(jnp.int32)

def group_attention(packed, q_weight, k_weight, v_weight, out_weight, position_bias):
    normed, lengths = packed
    row_count = normed.shape[0]
    queries = low_back(low(matrix_product(normed, q_weight))).reshape(row_count, HEADS, DH)
    key_heads = low_back(low(matrix_product(normed, k_weight))).reshape(row_count, HEADS, DH)
    value_heads = low_back(low(matrix_product(normed, v_weight))).reshape(row_count, HEADS, DH)
    places = jnp.arange(row_count, dtype=jnp.int32)
    bounds = jnp.cumsum(lengths).astype(jnp.int32)[:-1]
    documents = lax.optimization_barrier(jnp.sum((places[:, None] >= bounds[None, :]).astype(jnp.int32), axis=1))
    same_doc = documents[:, None] == documents[None, :]
    buckets = bucket_of(places[None, :] - places[:, None])
    bias_full = jnp.transpose(position_bias[buckets], (2, 0, 1))
    scores = jnp.einsum('qhd,khd->hqk', queries, key_heads, precision=lax.Precision.HIGHEST) * DH ** (-0.5) + bias_full
    scores = jnp.where(same_doc[None], low_back(scores), NEGATIVE)
    weights = low(jax.nn.softmax(scores, axis=-1))
    context = jnp.einsum('hqk,khd->qhd', weights, value_heads, precision=lax.Precision.HIGHEST).reshape(row_count, HEADS * DH)
    context = low_back(low(context))
    return matrix_product(context, out_weight)

def one_expert(packed):
    expert_rows, up_matrix, down_matrix = packed
    pre_active = low_back(matrix_product(expert_rows, up_matrix))
    return matrix_product(low(jax.nn.gelu(pre_active, approximate=True)), down_matrix)

def forward(doc_lengths, expert_route, hidden_in, norm1_gain, q_weight, k_weight, v_weight, out_weight, position_bias, norm2_gain, router_weight, expert_up, expert_down):
    first_normed = low(rms_norm(hidden_in, norm1_gain))

    def one_group(packed):
        return group_attention(packed, q_weight, k_weight, v_weight, out_weight, position_bias)
    attended = lax.map(jax.checkpoint(one_group), (first_normed.reshape(N_DP, TOK_DP, D), doc_lengths))
    attended = low_back(attended.reshape(TOKENS, D))
    middle = hidden_in + attended
    second_normed = low(rms_norm(middle, norm2_gain))
    router_probs = jax.nn.softmax(matrix_product(second_normed, router_weight), axis=-1)
    routes_flat = expert_route[:, 0].astype(jnp.int32)
    chosen = routes_flat[:, None] == jnp.arange(EXPERTS, dtype=jnp.int32)[None, :]
    gate_value = lax.optimization_barrier(jnp.sum(jnp.where(chosen, router_probs, 0.0), axis=1))
    counts = jnp.cumsum(chosen.astype(jnp.int32).reshape(N_DP, TOK_DP, EXPERTS), axis=1).astype(jnp.int32)
    counts = counts.reshape(TOKENS, EXPERTS)
    rank_within = lax.optimization_barrier(jnp.sum(jnp.where(chosen, counts, 0), axis=1)).astype(jnp.int32) - 1
    group_index = jnp.arange(TOKENS, dtype=jnp.int32) // TOK_DP
    slot_index = (routes_flat * (N_DP * CAP) + group_index * CAP + rank_within).astype(jnp.int32)
    buffer = jnp.zeros((EXPERTS * N_DP * CAP, D), jnp.float32).at[slot_index].add(second_normed)
    buffer = buffer.reshape(EXPERTS, N_DP * CAP, D)
    up_full = jnp.transpose(expert_up.reshape(EXPERTS, 2, D, FF // 2), (0, 2, 1, 3)).reshape(EXPERTS, D, FF)
    down_full = expert_down.reshape(EXPERTS, FF, D)
    expert_rows = lax.map(jax.checkpoint(one_expert), (buffer, up_full, down_full)).reshape(EXPERTS * N_DP * CAP, D)
    expert_out = low_back(expert_rows[slot_index])
    return middle + gate_value[:, None] * expert_out

def reference(hidden_in, norm1_gain, q_weight, k_weight, v_weight, out_weight, position_bias, norm2_gain, router_weight, expert_up, expert_down, doc_lengths, expert_route, out_grad):
    floats = (hidden_in.astype(jnp.float32), norm1_gain.astype(jnp.float32), q_weight.astype(jnp.float32), k_weight.astype(jnp.float32), v_weight.astype(jnp.float32), out_weight.astype(jnp.float32), position_bias.astype(jnp.float32), norm2_gain.astype(jnp.float32), router_weight.astype(jnp.float32), expert_up.astype(jnp.float32), expert_down.astype(jnp.float32))
    result, pullback = jax.vjp(partial(forward, doc_lengths, expert_route), *floats)
    gradients = pullback(out_grad.astype(jnp.float32))
    return (result.astype(jnp.bfloat16), gradients[0], gradients[1], gradients[2], gradients[3], gradients[4], gradients[5], gradients[6], gradients[7], gradients[8], gradients[9], gradients[10])
```

```python
from functools import partial

import jax
import jax.numpy as jnp
from jax import lax
from jax.sharding import PartitionSpec as P

DH = 64


EPSILON = 1e-06
NEGATIVE = -1e30
LIMITS = (12, 16, 23, 32, 46, 64, 91)


def rms_norm(values, gain_vector):
    return (
        values
        * lax.rsqrt(jnp.mean(values * values, axis=-1, keepdims=True) + EPSILON)
        * gain_vector
    )


def matmul(first_operand, second_operand):
    return jnp.dot(first_operand, second_operand, preferred_element_type=jnp.float32)


def contract_rows(first_operand, second_operand, precision=None):
    return lax.dot_general(
        first_operand,
        second_operand,
        (((0,), (0,)), ((), ())),
        precision=precision,
        preferred_element_type=jnp.float32,
    )


def contract_cols(first_operand, second_operand, precision=None):
    return lax.dot_general(
        first_operand,
        second_operand,
        (((1,), (1,)), ((), ())),
        precision=precision,
        preferred_element_type=jnp.float32,
    )


def bucket_of(offset):
    distance = jnp.abs(offset)
    beyond = jnp.zeros_like(distance)
    for boundary in LIMITS:
        beyond = beyond + (distance >= boundary).astype(jnp.int32)
    near_far = jnp.where(distance < 8, distance, 8 + beyond)
    return near_far + 16 * (offset > 0).astype(jnp.int32)


def expand_bias(bias_table, group_rows):
    offsets = jnp.arange(2 * group_rows - 1, dtype=jnp.int32) - (group_rows - 1)
    labels = jnp.arange(bias_table.shape[0], dtype=jnp.int32)
    bucket_picks = (bucket_of(offsets)[:, None] == labels[None, :]).astype(jnp.float32)
    per_offset = jnp.dot(
        bucket_picks,
        bias_table,
        precision=lax.Precision.HIGHEST,
        preferred_element_type=jnp.float32,
    )
    head_count = bias_table.shape[1]
    padded_line = jnp.pad(jnp.transpose(per_offset), ((0, 0), (0, 1)))
    tiled_line = jnp.broadcast_to(padded_line[:, None, :], (head_count, group_rows, 2 * group_rows))
    tiled_line = tiled_line.reshape(head_count, 2 * group_rows * group_rows)
    skewed = tiled_line[:, : group_rows * (2 * group_rows - 1)].reshape(
        head_count, group_rows, 2 * group_rows - 1
    )
    return skewed[:, :, group_rows - 1 :]


def spread(values):
    return lax.all_gather(values, "tensor", axis=0, tiled=True)


def swap_cores(values):
    return lax.ppermute(values, "tensor", perm=[(0, 1), (1, 0)])


def pick(values, index, axis=0):
    return lax.dynamic_index_in_dim(values, index, axis, keepdims=False)


def collect(values):
    core = lax.axis_index("tensor")
    halves = values.reshape(2, values.shape[0] // 2, values.shape[1])
    arrived = swap_cores(pick(halves, 1 - core).astype(jnp.bfloat16))
    return pick(halves, core) + arrived.astype(jnp.float32)


def dp_bits():
    return lax.axis_size("dp").bit_length() - 1


def partner_swap(values, bit):
    count = lax.axis_size("dp")
    return lax.ppermute(values, "dp", perm=[(i, i ^ (1 << bit)) for i in range(count)])


def own_bit(bit):
    return lax.rem(lax.div(lax.axis_index("dp"), 1 << bit), 2)


def gather_blocks(block, order):
    held = []
    for bit in order:
        axis = sum(1 for other in held if other > bit)
        arrived = partner_swap(block, bit)
        block = jnp.where(
            own_bit(bit) == 1,
            jnp.stack([arrived, block], axis=axis),
            jnp.stack([block, arrived], axis=axis),
        )
        held.append(bit)
    return block.reshape((-1,) + block.shape[len(order) :])


def scatter_blocks(blocks, order):
    left = list(reversed(range(len(order))))
    blocks = blocks.reshape((2,) * len(order) + blocks.shape[1:])
    for bit in order:
        axis = left.index(bit)
        mine = own_bit(bit)
        sent = pick(blocks, 1 - mine, axis).astype(jnp.bfloat16)
        kept = pick(blocks, mine, axis).astype(jnp.float32)
        blocks = kept + partner_swap(sent, bit).astype(jnp.float32)
        left.remove(bit)
    return blocks


def to_expert(outgoing):
    doubled = jnp.repeat(outgoing, 2, axis=0)
    arrived = lax.all_to_all(doubled, "dp", split_axis=0, concat_axis=0, tiled=True)
    rows = lax.all_gather(arrived.reshape(-1, outgoing.shape[2]), "tensor", axis=0)
    half = outgoing.shape[2] // 2
    first = jnp.concatenate([rows[0, :, :half], rows[1, :, :half]], axis=1)
    second = jnp.concatenate([rows[0, :, half:], rows[1, :, half:]], axis=1)
    return first, second


def from_expert(first, second, capacity):
    core = lax.axis_index("tensor")
    half = first.shape[1] // 2
    parts = [
        jnp.concatenate(
            [first[:, c * half : (c + 1) * half], second[:, c * half : (c + 1) * half]], axis=1
        )
        for c in range(2)
    ]
    sent = jnp.where(core == 0, parts[1], parts[0]).astype(jnp.bfloat16)
    kept = jnp.where(core == 0, parts[0], parts[1])
    summed = (kept + swap_cores(sent).astype(jnp.float32)).astype(jnp.bfloat16)
    sources = first.shape[0] // capacity
    returned = lax.all_to_all(
        summed.reshape(sources, capacity, 2 * half), "dp", split_axis=0, concat_axis=0, tiled=True
    ).astype(jnp.float32)
    return jnp.sum(returned.reshape(sources // 2, 2, capacity, 2 * half), axis=1).reshape(
        -1, 2 * half
    )


def own_columns(rows):
    core = lax.axis_index("tensor")
    half = rows.shape[1] // 2
    split = rows.astype(jnp.bfloat16).reshape(2, rows.shape[0] // 2, rows.shape[1])
    arrived = swap_cores(pick(split, 1 - core))
    kept = pick(split, core)
    left = jnp.where(core == 0, kept, arrived).astype(jnp.float32)
    right = jnp.where(core == 0, arrived, kept).astype(jnp.float32)
    return (
        jnp.concatenate([left[:, :half], right[:, :half]], axis=1),
        jnp.concatenate([left[:, half:], right[:, half:]], axis=1),
    )


def block_scores(query_block, key_heads, bias_block, mask_block):
    raw_scores = (
        jnp.einsum("qhd,khd->hqk", query_block, key_heads, preferred_element_type=jnp.float32)
        * DH ** (-0.5)
        + bias_block
    )
    return jnp.where(mask_block[None], raw_scores, NEGATIVE)


def shards(
    hidden_in,
    norm1_gain,
    q_weight,
    k_weight,
    v_weight,
    out_weight,
    position_bias,
    norm2_gain,
    router_weight,
    expert_up,
    expert_down,
    doc_lengths,
    expert_route,
    out_grad,
):
    half_rows = hidden_in.shape[0]
    group_rows = half_rows * lax.axis_size("tensor")
    own_start = lax.axis_index("tensor") * half_rows
    model_width = hidden_in.shape[1]
    expert_count = router_weight.shape[1]
    capacity = max(2, 5 * group_rows // (4 * expert_count))
    heads_here = position_bias.shape[1]
    score_scale = DH ** (-0.5)
    own_rows = hidden_in.astype(jnp.float32)
    first_normed = rms_norm(own_rows, norm1_gain).astype(jnp.bfloat16)
    down = list(reversed(range(dp_bits())))
    down_other = down[:-2] + [down[-1], down[-2]]
    up, up_other = down[::-1], down_other[::-1]
    weight_rows = q_weight.shape[0]
    qk_blocks = gather_blocks(jnp.stack([q_weight, k_weight]), down)
    vo_blocks = gather_blocks(jnp.stack([v_weight, out_weight.T]), down_other)
    q_full = qk_blocks[:, 0].reshape(model_width, -1)
    k_full = qk_blocks[:, 1].reshape(model_width, -1)
    v_full = vo_blocks[:, 0].reshape(model_width, -1)
    o_rows = vo_blocks[:, 1].reshape(model_width, -1)
    first_all = spread(first_normed)
    queries = matmul(first_all, q_full).astype(jnp.bfloat16)
    key_rows = matmul(first_all, k_full).astype(jnp.bfloat16)
    value_rows = matmul(first_all, v_full).astype(jnp.bfloat16)
    query_heads = queries.reshape(group_rows, heads_here, DH)
    key_heads = key_rows.reshape(group_rows, heads_here, DH)
    value_heads = value_rows.reshape(group_rows, heads_here, DH)
    places = jnp.arange(group_rows, dtype=jnp.int32)
    bounds = jnp.cumsum(doc_lengths[0])[:-1]
    documents = jnp.sum((places[:, None] >= bounds[None, :]).astype(jnp.int32), axis=1)
    same_doc = documents[:, None] == documents[None, :]

    def bias_of(bias_table):
        return expand_bias(bias_table, group_rows)

    bias_full = bias_of(position_bias)
    scores = block_scores(query_heads, key_heads, bias_full, same_doc)
    top_score = jnp.max(scores, axis=-1, keepdims=True)
    exponent = jnp.exp(scores - top_score)
    total_mass = jnp.sum(exponent, axis=-1, keepdims=True)
    weights = (exponent / total_mass).astype(jnp.bfloat16)
    context_blocks = jnp.einsum(
        "hqk,khd->qhd", weights, value_heads, preferred_element_type=jnp.float32
    ).astype(jnp.bfloat16)
    log_blocks = top_score + jnp.log(total_mass)
    context = context_blocks.reshape(group_rows, heads_here * DH)
    attended = collect(contract_cols(context, o_rows))
    middle = own_rows + attended
    second_normed = rms_norm(middle, norm2_gain).astype(jnp.bfloat16)
    second_float = second_normed.astype(jnp.float32)
    logits = jnp.dot(
        second_float,
        router_weight,
        precision=lax.Precision.HIGHEST,
        preferred_element_type=jnp.float32,
    )
    router_probs = jax.nn.softmax(logits, axis=-1)
    routes_flat = expert_route[:, 0]
    chosen = routes_flat[:, None] == jnp.arange(expert_count, dtype=jnp.int32)[None, :]
    chosen_own = lax.dynamic_slice_in_dim(chosen, own_start, half_rows, 0)
    gate_value = jnp.sum(jnp.where(chosen_own, router_probs, 0.0), axis=1)
    counts = jnp.cumsum(chosen.astype(jnp.int32), axis=0)
    rank_within = jnp.sum(jnp.where(chosen, counts, 0), axis=1) - 1
    slot_index = routes_flat * capacity + rank_within
    slot_owner = (
        jnp.full((expert_count * capacity,), group_rows, jnp.int32).at[slot_index].set(places)
    )
    d_result = out_grad.astype(jnp.float32)
    d_expert = (gate_value[:, None] * d_result).astype(jnp.bfloat16)
    both_all = spread(jnp.concatenate([second_normed, d_expert], axis=1))
    column_half = model_width // 2
    both_half = jnp.where(
        lax.axis_index("tensor") == 0,
        jnp.concatenate(
            [both_all[:, :column_half], both_all[:, model_width : model_width + column_half]],
            axis=1,
        ),
        jnp.concatenate(
            [both_all[:, column_half:model_width], both_all[:, model_width + column_half :]],
            axis=1,
        ),
    )
    zero_row = jnp.zeros((1, model_width), jnp.bfloat16)
    outgoing = jnp.take(jnp.concatenate([both_half, zero_row], axis=0), slot_owner, axis=0)
    incoming, d_incoming = to_expert(outgoing.reshape(expert_count, capacity, model_width))
    pre_active = matmul(incoming, expert_up[0])
    active = jax.nn.gelu(pre_active, approximate=True).astype(jnp.bfloat16)
    partial_rows = matmul(active, expert_down[0])
    d_active = contract_cols(d_incoming, expert_down[0])
    _, gelu_pull = jax.vjp(partial(jax.nn.gelu, approximate=True), pre_active)
    d_pre = gelu_pull(d_active)[0].astype(jnp.bfloat16)
    d_rows = contract_cols(d_pre, expert_up[0])
    returned = from_expert(partial_rows, d_rows, capacity)
    down_grad = contract_rows(active, d_incoming)
    up_grad = contract_rows(incoming, d_pre)
    expert_out, d_second = own_columns(jnp.take(returned, slot_index, axis=0))
    hidden_out = (middle + gate_value[:, None] * expert_out).astype(jnp.bfloat16)
    d_gate = jnp.sum(d_result * expert_out, axis=1)
    d_logits = router_probs * (
        jnp.where(chosen_own, d_gate[:, None], 0.0) - (gate_value * d_gate)[:, None]
    )
    d_second = d_second + contract_cols(d_logits, router_weight, lax.Precision.HIGHEST)
    router_grad = contract_rows(second_float, d_logits, lax.Precision.HIGHEST)
    _, norm_pull = jax.vjp(rms_norm, middle, norm2_gain)
    d_middle_norm, second_gain_grad = norm_pull(d_second)
    d_middle = d_result + d_middle_norm
    d_attended = spread(d_middle.astype(jnp.bfloat16))
    out_rows_grad = contract_rows(d_attended, context)
    o_grad = scatter_blocks(out_rows_grad.reshape(-1, weight_rows, heads_here * DH), up).T
    d_context = matmul(d_attended, o_rows).astype(jnp.bfloat16)
    context_heads = d_context.reshape(group_rows, heads_here, DH)
    scores = block_scores(query_heads, key_heads, bias_full, same_doc)
    weights = jnp.exp(scores - log_blocks)
    d_weights = jnp.einsum(
        "qhd,khd->hqk", context_heads, value_heads, preferred_element_type=jnp.float32
    )
    d_scores = (
        weights * (d_weights - jnp.sum(weights * d_weights, axis=-1, keepdims=True))
    ).astype(jnp.bfloat16)
    query_grads = (
        jnp.einsum("hqk,khd->qhd", d_scores, key_heads, preferred_element_type=jnp.float32)
        * score_scale
    )
    d_key_sum = (
        jnp.einsum("hqk,qhd->khd", d_scores, query_heads, preferred_element_type=jnp.float32)
        * score_scale
    )
    d_value_sum = jnp.einsum(
        "hqk,qhd->khd",
        weights.astype(jnp.bfloat16),
        context_heads,
        preferred_element_type=jnp.float32,
    )
    d_queries = query_grads.reshape(group_rows, heads_here * DH).astype(jnp.bfloat16)
    d_keys = d_key_sum.reshape(group_rows, heads_here * DH).astype(jnp.bfloat16)
    d_values = d_value_sum.reshape(group_rows, heads_here * DH).astype(jnp.bfloat16)
    _, bias_pull = jax.vjp(bias_of, position_bias)
    bias_grad = bias_pull(d_scores.astype(jnp.float32))[0]
    query_matrix_grad = contract_rows(first_all, d_queries)
    key_matrix_grad = contract_rows(first_all, d_keys)
    value_matrix_grad = contract_rows(first_all, d_values)
    d_first = (
        contract_cols(d_queries, q_full)
        + contract_cols(d_keys, k_full)
        + contract_cols(d_values, v_full)
    )
    d_first = collect(d_first)
    _, first_pull = jax.vjp(rms_norm, own_rows, norm1_gain)
    d_own_norm, first_gain_grad = first_pull(d_first)
    input_grad = d_middle + d_own_norm
    joint = jnp.concatenate(
        [
            grad.reshape(-1, weight_rows, heads_here * DH)
            for grad in (query_matrix_grad, key_matrix_grad, value_matrix_grad)
        ],
        axis=1,
    )
    cut = joint.shape[1] // 2
    joint_own = jnp.concatenate(
        [scatter_blocks(joint[:, :cut], up), scatter_blocks(joint[:, cut:], up_other)], axis=0
    )
    q_grad, k_grad, v_grad = (
        joint_own[i * weight_rows : (i + 1) * weight_rows] for i in range(3)
    )
    small = jnp.concatenate(
        [
            first_gain_grad.reshape(-1),
            second_gain_grad.reshape(-1),
            router_grad.T.reshape(-1),
            bias_grad.reshape(-1),
        ]
    )
    for bit in range(dp_bits()):
        small = small + partner_swap(small, bit)
    bias_own = small[-bias_grad.size :].reshape(bias_grad.shape)
    shared = small[: -bias_grad.size]
    shared = shared + swap_cores(shared)
    gain_one = shared[:model_width]
    gain_two = shared[model_width : 2 * model_width]
    router_total = shared[2 * model_width :].reshape(expert_count, model_width).T
    return (
        hidden_out,
        input_grad,
        gain_one,
        q_grad,
        k_grad,
        v_grad,
        o_grad,
        bias_own,
        gain_two,
        router_total,
        up_grad[None],
        down_grad[None],
    )


def solution(mesh):
    return jax.shard_map(
        shards,
        mesh=mesh,
        in_specs=(
            P(("dp", "tensor"), None),
            P(),
            P("dp", "tensor"),
            P("dp", "tensor"),
            P("dp", "tensor"),
            P("tensor", "dp"),
            P(None, "tensor"),
            P(),
            P(),
            P("dp", None, "tensor"),
            P("dp", "tensor", None),
            P("dp", None),
            P("dp", None),
            P(("dp", "tensor"), None),
        ),
        out_specs=(
            P(("dp", "tensor"), None),
            P(("dp", "tensor"), None),
            P(),
            P("dp", "tensor"),
            P("dp", "tensor"),
            P("dp", "tensor"),
            P("tensor", "dp"),
            P(None, "tensor"),
            P(),
            P(),
            P("dp", None, "tensor"),
            P("dp", "tensor", None),
        ),
        check_vma=False,
    )
```

```python
from functools import partial

import jax
import jax.numpy as jnp
from jax import lax
from jax.sharding import PartitionSpec as P

DH = 64


EPSILON = 1e-06
NEGATIVE = -1e30
LIMITS = (12, 16, 23, 32, 46, 64, 91)


def rms_norm(values, gain_vector):
    return (
        values
        * lax.rsqrt(jnp.mean(values * values, axis=-1, keepdims=True) + EPSILON)
        * gain_vector
    )


def matmul(first_operand, second_operand):
    return jnp.dot(first_operand, second_operand, preferred_element_type=jnp.float32)


def contract_rows(first_operand, second_operand, precision=None):
    return lax.dot_general(
        first_operand,
        second_operand,
        (((0,), (0,)), ((), ())),
        precision=precision,
        preferred_element_type=jnp.float32,
    )


def contract_cols(first_operand, second_operand, precision=None):
    return lax.dot_general(
        first_operand,
        second_operand,
        (((1,), (1,)), ((), ())),
        precision=precision,
        preferred_element_type=jnp.float32,
    )


def bucket_of(offset):
    distance = jnp.abs(offset)
    beyond = jnp.zeros_like(distance)
    for boundary in LIMITS:
        beyond = beyond + (distance >= boundary).astype(jnp.int32)
    near_far = jnp.where(distance < 8, distance, 8 + beyond)
    return near_far + 16 * (offset > 0).astype(jnp.int32)


def expand_bias(bias_table, group_rows):
    offsets = jnp.arange(2 * group_rows - 1, dtype=jnp.int32) - (group_rows - 1)
    labels = jnp.arange(bias_table.shape[0], dtype=jnp.int32)
    bucket_picks = (bucket_of(offsets)[:, None] == labels[None, :]).astype(jnp.float32)
    per_offset = jnp.dot(
        bucket_picks,
        bias_table,
        precision=lax.Precision.HIGHEST,
        preferred_element_type=jnp.float32,
    )
    head_count = bias_table.shape[1]
    padded_line = jnp.pad(jnp.transpose(per_offset), ((0, 0), (0, 1)))
    tiled_line = jnp.broadcast_to(padded_line[:, None, :], (head_count, group_rows, 2 * group_rows))
    tiled_line = tiled_line.reshape(head_count, 2 * group_rows * group_rows)
    skewed = tiled_line[:, : group_rows * (2 * group_rows - 1)].reshape(
        head_count, group_rows, 2 * group_rows - 1
    )
    return skewed[:, :, group_rows - 1 :]


def spread(values):
    return lax.all_gather(values, "tensor", axis=0, tiled=True)


def swap_cores(values):
    return lax.ppermute(values, "tensor", perm=[(0, 1), (1, 0)])


def pick(values, index, axis=0):
    return lax.dynamic_index_in_dim(values, index, axis, keepdims=False)


def collect(values):
    core = lax.axis_index("tensor")
    halves = values.reshape(2, values.shape[0] // 2, values.shape[1])
    arrived = swap_cores(pick(halves, 1 - core).astype(jnp.bfloat16))
    return pick(halves, core) + arrived.astype(jnp.float32)


def dp_bits():
    return lax.axis_size("dp").bit_length() - 1


def partner_swap(values, bit):
    count = lax.axis_size("dp")
    return lax.ppermute(values, "dp", perm=[(i, i ^ (1 << bit)) for i in range(count)])


def own_bit(bit):
    return lax.rem(lax.div(lax.axis_index("dp"), 1 << bit), 2)


def gather_blocks(block, order):
    held = []
    early = block
    for bit in order:
        early = block
        axis = sum(1 for other in held if other > bit)
        arrived = partner_swap(block, bit)
        block = jnp.where(
            own_bit(bit) == 1,
            jnp.stack([arrived, block], axis=axis),
            jnp.stack([block, arrived], axis=axis),
        )
        held.append(bit)
    return block.reshape((-1,) + block.shape[len(order) :]), early


def zero_after(values):
    first = values[(slice(0, 1),) * values.ndim].reshape(())
    return jnp.minimum(jnp.abs(first.astype(jnp.float32)), 0.0)


def scatter_blocks(blocks, order):
    left = list(reversed(range(len(order))))
    blocks = blocks.reshape((2,) * len(order) + blocks.shape[1:])
    early = None
    for bit in order:
        axis = left.index(bit)
        mine = own_bit(bit)
        sent = pick(blocks, 1 - mine, axis).astype(jnp.bfloat16)
        kept = pick(blocks, mine, axis).astype(jnp.float32)
        blocks = kept + partner_swap(sent, bit).astype(jnp.float32)
        left.remove(bit)
        early = blocks if early is None else early
    return blocks, early


def to_expert(outgoing):
    doubled = jnp.repeat(outgoing, 2, axis=0)
    arrived = lax.all_to_all(doubled, "dp", split_axis=0, concat_axis=0, tiled=True)
    mine = arrived.reshape(-1, outgoing.shape[2])
    other = swap_cores(mine)
    low = lax.axis_index("tensor") == 0
    rows = (jnp.where(low, mine, other), jnp.where(low, other, mine))
    half = outgoing.shape[2] // 2
    first = jnp.concatenate([rows[0][:, :half], rows[1][:, :half]], axis=1)
    second = jnp.concatenate([rows[0][:, half:], rows[1][:, half:]], axis=1)
    return first, second


def from_expert(first, second, capacity):
    core = lax.axis_index("tensor")
    half = first.shape[1] // 2
    parts = [
        jnp.concatenate(
            [first[:, c * half : (c + 1) * half], second[:, c * half : (c + 1) * half]], axis=1
        )
        for c in range(2)
    ]
    sent = jnp.where(core == 0, parts[1], parts[0]).astype(jnp.bfloat16)
    kept = jnp.where(core == 0, parts[0], parts[1])
    summed = (kept + swap_cores(sent).astype(jnp.float32)).astype(jnp.bfloat16)
    sources = first.shape[0] // capacity
    returned = lax.all_to_all(
        summed.reshape(sources, capacity, 2 * half), "dp", split_axis=0, concat_axis=0, tiled=True
    ).astype(jnp.float32)
    return jnp.sum(returned.reshape(sources // 2, 2, capacity, 2 * half), axis=1).reshape(
        -1, 2 * half
    )


def own_columns(rows):
    core = lax.axis_index("tensor")
    half = rows.shape[1] // 2
    split = rows.astype(jnp.bfloat16).reshape(2, rows.shape[0] // 2, rows.shape[1])
    arrived = swap_cores(pick(split, 1 - core))
    kept = pick(split, core)
    left = jnp.where(core == 0, kept, arrived).astype(jnp.float32)
    right = jnp.where(core == 0, arrived, kept).astype(jnp.float32)
    return (
        jnp.concatenate([left[:, :half], right[:, :half]], axis=1),
        jnp.concatenate([left[:, half:], right[:, half:]], axis=1),
    )


def block_scores(query_block, key_heads, bias_block, mask_block):
    raw_scores = (
        jnp.einsum("qhd,khd->hqk", query_block, key_heads, preferred_element_type=jnp.float32)
        * DH ** (-0.5)
        + bias_block
    )
    return jnp.where(mask_block[None], raw_scores, NEGATIVE)


def shards(
    hidden_in,
    norm1_gain,
    q_weight,
    k_weight,
    v_weight,
    out_weight,
    position_bias,
    norm2_gain,
    router_weight,
    expert_up,
    expert_down,
    doc_lengths,
    expert_route,
    out_grad,
):
    half_rows = hidden_in.shape[0]
    group_rows = half_rows * lax.axis_size("tensor")
    own_start = lax.axis_index("tensor") * half_rows
    model_width = hidden_in.shape[1]
    expert_count = router_weight.shape[1]
    capacity = max(2, 5 * group_rows // (4 * expert_count))
    heads_here = position_bias.shape[1]
    score_scale = DH ** (-0.5)
    own_rows = hidden_in.astype(jnp.float32)
    first_normed = rms_norm(own_rows, norm1_gain).astype(jnp.bfloat16)
    down = list(reversed(range(dp_bits())))
    down_other = down[:-2] + [down[-1], down[-2]]
    up, up_other = down[::-1], down_other[::-1]
    weight_rows = q_weight.shape[0]
    qk_blocks, qk_early = gather_blocks(jnp.stack([q_weight, k_weight]), down)
    vo_blocks, _ = gather_blocks(jnp.stack([v_weight, out_weight.T]), down_other)
    q_full = qk_blocks[:, 0].reshape(model_width, -1)
    k_full = qk_blocks[:, 1].reshape(model_width, -1)
    v_full = vo_blocks[:, 0].reshape(model_width, -1)
    o_rows = vo_blocks[:, 1].reshape(model_width, -1)
    first_all = spread(first_normed)
    queries = matmul(first_all, q_full).astype(jnp.bfloat16)
    key_rows = matmul(first_all, k_full).astype(jnp.bfloat16)
    value_rows = matmul(first_all, v_full).astype(jnp.bfloat16)
    query_heads = queries.reshape(group_rows, heads_here, DH)
    key_heads = key_rows.reshape(group_rows, heads_here, DH)
    value_heads = value_rows.reshape(group_rows, heads_here, DH)
    places = jnp.arange(group_rows, dtype=jnp.int32)
    bounds = jnp.cumsum(doc_lengths[0])[:-1]
    documents = jnp.sum((places[:, None] >= bounds[None, :]).astype(jnp.int32), axis=1)
    same_doc = documents[:, None] == documents[None, :]

    def bias_of(bias_table):
        return expand_bias(bias_table, group_rows)

    bias_full = bias_of(position_bias + zero_after(qk_early))
    scores = block_scores(query_heads, key_heads, bias_full, same_doc)
    top_score = jnp.max(scores, axis=-1, keepdims=True)
    exponent = jnp.exp(scores - top_score)
    total_mass = jnp.sum(exponent, axis=-1, keepdims=True)
    weights = (exponent / total_mass).astype(jnp.bfloat16)
    context_blocks = jnp.einsum(
        "hqk,khd->qhd", weights, value_heads, preferred_element_type=jnp.float32
    ).astype(jnp.bfloat16)
    log_blocks = top_score + jnp.log(total_mass)
    context = context_blocks.reshape(group_rows, heads_here * DH)
    attended = collect(contract_cols(context, o_rows))
    middle = own_rows + attended
    second_normed = rms_norm(middle, norm2_gain).astype(jnp.bfloat16)
    second_float = second_normed.astype(jnp.float32)
    logits = jnp.dot(
        second_float,
        router_weight,
        precision=lax.Precision.HIGHEST,
        preferred_element_type=jnp.float32,
    )
    router_probs = jax.nn.softmax(logits, axis=-1)
    routes_flat = expert_route[:, 0]
    chosen = routes_flat[:, None] == jnp.arange(expert_count, dtype=jnp.int32)[None, :]
    chosen_own = lax.dynamic_slice_in_dim(chosen, own_start, half_rows, 0)
    gate_value = jnp.sum(jnp.where(chosen_own, router_probs, 0.0), axis=1)
    counts = jnp.cumsum(chosen.astype(jnp.int32), axis=0)
    rank_within = jnp.sum(jnp.where(chosen, counts, 0), axis=1) - 1
    slot_index = routes_flat * capacity + rank_within
    slot_owner = (
        jnp.full((expert_count * capacity,), group_rows, jnp.int32).at[slot_index].set(places)
    )
    d_result = out_grad.astype(jnp.float32)
    d_expert = (gate_value[:, None] * d_result).astype(jnp.bfloat16)
    both_all = spread(jnp.concatenate([second_normed, d_expert], axis=1))
    column_half = model_width // 2
    both_half = jnp.where(
        lax.axis_index("tensor") == 0,
        jnp.concatenate(
            [both_all[:, :column_half], both_all[:, model_width : model_width + column_half]],
            axis=1,
        ),
        jnp.concatenate(
            [both_all[:, column_half:model_width], both_all[:, model_width + column_half :]],
            axis=1,
        ),
    )
    zero_row = jnp.zeros((1, model_width), jnp.bfloat16)
    outgoing = jnp.take(jnp.concatenate([both_half, zero_row], axis=0), slot_owner, axis=0)
    incoming, d_incoming = to_expert(outgoing.reshape(expert_count, capacity, model_width))
    pre_active = matmul(incoming, expert_up[0])
    active = jax.nn.gelu(pre_active, approximate=True).astype(jnp.bfloat16)
    partial_rows = matmul(active, expert_down[0])
    d_active = contract_cols(d_incoming, expert_down[0])
    _, gelu_pull = jax.vjp(partial(jax.nn.gelu, approximate=True), pre_active)
    d_pre = gelu_pull(d_active)[0].astype(jnp.bfloat16)
    d_rows = contract_cols(d_pre, expert_up[0])
    returned = from_expert(partial_rows, d_rows, capacity)
    down_grad = contract_rows(active, d_incoming)
    expert_out, d_second = own_columns(jnp.take(returned, slot_index, axis=0))
    hidden_out = (middle + gate_value[:, None] * expert_out).astype(jnp.bfloat16)
    d_gate = jnp.sum(d_result * expert_out, axis=1)
    d_logits = router_probs * (
        jnp.where(chosen_own, d_gate[:, None], 0.0) - (gate_value * d_gate)[:, None]
    )
    d_second = d_second + contract_cols(d_logits, router_weight, lax.Precision.HIGHEST)
    router_grad = contract_rows(second_float, d_logits, lax.Precision.HIGHEST)
    _, norm_pull = jax.vjp(rms_norm, middle, norm2_gain)
    d_middle_norm, second_gain_grad = norm_pull(d_second)
    d_middle = d_result + d_middle_norm
    d_attended = spread(d_middle.astype(jnp.bfloat16))
    out_rows_grad = contract_rows(d_attended, context)
    o_own, _ = scatter_blocks(out_rows_grad.reshape(-1, weight_rows, heads_here * DH), up)
    o_grad = o_own.T
    d_context = matmul(d_attended, o_rows).astype(jnp.bfloat16)
    context_heads = d_context.reshape(group_rows, heads_here, DH)
    scores = block_scores(query_heads, key_heads, bias_full, same_doc)
    weights = jnp.exp(scores - log_blocks)
    d_weights = jnp.einsum(
        "qhd,khd->hqk", context_heads, value_heads, preferred_element_type=jnp.float32
    )
    d_scores = (
        weights * (d_weights - jnp.sum(weights * d_weights, axis=-1, keepdims=True))
    ).astype(jnp.bfloat16)
    query_grads = (
        jnp.einsum("hqk,khd->qhd", d_scores, key_heads, preferred_element_type=jnp.float32)
        * score_scale
    )
    d_key_sum = (
        jnp.einsum("hqk,qhd->khd", d_scores, query_heads, preferred_element_type=jnp.float32)
        * score_scale
    )
    d_value_sum = jnp.einsum(
        "hqk,qhd->khd",
        weights.astype(jnp.bfloat16),
        context_heads,
        preferred_element_type=jnp.float32,
    )
    d_queries = query_grads.reshape(group_rows, heads_here * DH).astype(jnp.bfloat16)
    d_keys = d_key_sum.reshape(group_rows, heads_here * DH).astype(jnp.bfloat16)
    d_values = d_value_sum.reshape(group_rows, heads_here * DH).astype(jnp.bfloat16)
    query_matrix_grad = contract_rows(first_all, d_queries)
    key_matrix_grad = contract_rows(first_all, d_keys)
    value_matrix_grad = contract_rows(first_all, d_values)
    d_first = (
        contract_cols(d_queries, q_full)
        + contract_cols(d_keys, k_full)
        + contract_cols(d_values, v_full)
    )
    d_first = collect(d_first)
    _, first_pull = jax.vjp(rms_norm, own_rows, norm1_gain)
    d_own_norm, first_gain_grad = first_pull(d_first)
    input_grad = d_middle + d_own_norm
    joint = jnp.concatenate(
        [
            grad.reshape(-1, weight_rows, heads_here * DH)
            for grad in (query_matrix_grad, key_matrix_grad, value_matrix_grad)
        ],
        axis=1,
    )
    cut = joint.shape[1] // 2
    joint_first, early_first = scatter_blocks(joint[:, :cut], up)
    joint_second, early_second = scatter_blocks(joint[:, cut:], up_other)
    joint_own = jnp.concatenate([joint_first, joint_second], axis=0)
    _, bias_pull = jax.vjp(bias_of, position_bias)
    bias_grad = bias_pull(d_scores.astype(jnp.float32) + zero_after(early_first))[0]
    up_grad = contract_rows(incoming, d_pre + zero_after(early_second).astype(jnp.bfloat16))
    q_grad, k_grad, v_grad = (
        joint_own[i * weight_rows : (i + 1) * weight_rows] for i in range(3)
    )
    small = jnp.concatenate(
        [
            first_gain_grad.reshape(-1),
            second_gain_grad.reshape(-1),
            router_grad.T.reshape(-1),
            bias_grad.reshape(-1),
        ]
    )
    for bit in range(dp_bits()):
        small = small + partner_swap(small, bit)
    bias_own = small[-bias_grad.size :].reshape(bias_grad.shape)
    shared = small[: -bias_grad.size]
    shared = shared + swap_cores(shared)
    gain_one = shared[:model_width]
    gain_two = shared[model_width : 2 * model_width]
    router_total = shared[2 * model_width :].reshape(expert_count, model_width).T
    return (
        hidden_out,
        input_grad,
        gain_one,
        q_grad,
        k_grad,
        v_grad,
        o_grad,
        bias_own,
        gain_two,
        router_total,
        up_grad[None],
        down_grad[None],
    )


def solution(mesh):
    return jax.shard_map(
        shards,
        mesh=mesh,
        in_specs=(
            P(("dp", "tensor"), None),
            P(),
            P("dp", "tensor"),
            P("dp", "tensor"),
            P("dp", "tensor"),
            P("tensor", "dp"),
            P(None, "tensor"),
            P(),
            P(),
            P("dp", None, "tensor"),
            P("dp", "tensor", None),
            P("dp", None),
            P("dp", None),
            P(("dp", "tensor"), None),
        ),
        out_specs=(
            P(("dp", "tensor"), None),
            P(("dp", "tensor"), None),
            P(),
            P("dp", "tensor"),
            P("dp", "tensor"),
            P("dp", "tensor"),
            P("tensor", "dp"),
            P(None, "tensor"),
            P(),
            P(),
            P("dp", None, "tensor"),
            P("dp", "tensor", None),
        ),
        check_vma=False,
    )
```
